32 devices in a mesh: phi: 2 (over x), theta: 4 (over y, core), row: 4 (over z).
Axes of the slice: x: 2, y: 2, z: 4, core: 2. Of those that a mesh axis runs over, the one named last changes fastest.
Arguments:
- fields: float32 [8, 12, 1536, 512], P(None, 'row', 'phi', 'theta'), may hold values from -6 to 6
- kept_counts: int32 [512], replicated, may hold values from 1 to 384, as said below
Outputs:
- filtered: float32 [8, 12, 1536, 512], P(None, 'row', 'phi', 'theta')
The draws below stay inside these ranges and needn't reach their ends.
Inputs may be any that keep to these rules, and one draw needn't show every extreme that they name: `kept_counts`: modes 0 to count - 1 of a cap row are kept; some row reaches 384 in every draw.
All inputs are finite; a program needn't handle non-finite values.
Results may differ from the reference program's by a relative error of at most 0.00007.
Values sent between devices are 32-bit elements; how exact they have to be, the bound alone decides.
A program may use at most 64 MiB of HBM per device.

```python
import jax
import jax.numpy as jnp
from jax import lax

NPHI = 1536
KMAX = 384
FIELDS = 8
CAP_BANDS = 2
TH_DEV = 128
NTH = 512
NR = 12


def draw_kept_counts(key, part):
    cap_total = 2 * CAP_BANDS * TH_DEV
    values = jax.random.randint(jax.random.fold_in(key, 11), (cap_total,), 1, KMAX + 1)
    position = jax.random.randint(jax.random.fold_in(key, 12), (), 0, cap_total)
    return values.at[position].set(KMAX).astype(jnp.int32)


def levels(own_key, dims, cuts, low, high):
    level = 1.0
    for dim, blocks in cuts:
        steps = jax.random.uniform(jax.random.fold_in(jax.random.fold_in(own_key, 6), dim), (blocks,), jnp.float32, low / len(cuts), high / len(cuts))
        level = level * jnp.repeat(jnp.exp(steps), dims[dim] // blocks).reshape((-1,) + (1,) * (len(dims) - 1 - dim))
    return level


def gaussian(key, shape, deviation, bound, cuts=(), held_as=jnp.bfloat16):
    result = deviation * jax.random.normal(key, shape, jnp.float32)
    if cuts:
        result = result * levels(key, shape, cuts, -0.22, 0.18)
    return jnp.clip(result, -bound, bound).astype(held_as)


def setup_inputs(seed: int = 0) -> dict:
    arg_keys = jax.random.split(jax.random.key(seed), 3)
    return {
        "fields": gaussian(arg_keys[0], (FIELDS, NR, NPHI, NTH), 1.0, 6.0, ((1, 4), (2, 2), (3, 4)), jnp.float32),
        "kept_counts": draw_kept_counts(jax.random.fold_in(arg_keys[2], 71), 0),
    }


def reference(fields, kept_counts):
    cap_rows = CAP_BANDS * TH_DEV
    north = fields[:, :, :, :cap_rows]
    south = fields[:, :, :, NTH - cap_rows:]
    caps = jnp.concatenate([north, south], axis=3)
    wavenumber = jnp.arange(NPHI // 2 + 1, dtype=jnp.int32)
    keep = wavenumber[:, None] < kept_counts[None, :]

    def filter_field(field):
        spectrum = jnp.fft.rfft(field, axis=1)
        spectrum = jnp.where(keep[None, :, :], spectrum, 0.0)
        return jnp.fft.irfft(spectrum, n=NPHI, axis=1).astype(jnp.float32)

    smoothed = lax.map(filter_field, caps)
    middle = fields[:, :, :, cap_rows:NTH - cap_rows]
    return jnp.concatenate([smoothed[:, :, :, :cap_rows], middle, smoothed[:, :, :, cap_rows:]], axis=3)
```

```python
import functools
import math

import jax
import jax.numpy as jnp
import ml_dtypes
import numpy as np
from jax import lax
from jax.experimental import pallas as pl
from jax.experimental.pallas import tpu as pltpu
from jax.sharding import PartitionSpec as P

KMAX = 384
TILE = 128
LANES = 128


def tables(offset, span_rows, points, mode_count):
    azimuth = offset + jnp.arange(span_rows, dtype=jnp.int32)
    wavenumber = jnp.arange(mode_count, dtype=jnp.int32)
    phase_turns = azimuth[:, None] * wavenumber[None, :] % points
    angles = phase_turns.astype(jnp.float32) * (2.0 * math.pi / points)
    forward = jnp.concatenate([jnp.cos(angles), jnp.sin(angles)], axis=1)
    weight = jnp.where(wavenumber == 0, 1.0, 2.0).astype(jnp.float32) / points
    weight = jnp.concatenate([weight, weight])
    backward = (forward * weight[None, :]).T
    return (forward, backward)


def spectral(lines, row_counts):
    nfields, shells, local_points, rows_here = lines.shape
    n_phi = lax.axis_size("phi")
    points = local_points * n_phi
    highest = lax.Precision.HIGHEST
    groups = nfields * shells
    grouped = lines.reshape(groups, local_points, rows_here)
    line_counts = jnp.broadcast_to(row_counts[None, :], (groups, rows_here)).reshape(-1)
    phi_index = lax.axis_index("phi")
    forward, backward = tables(phi_index * local_points, local_points, points, KMAX)
    share_rows = forward.shape[1] // n_phi
    out = jnp.einsum(
        "pk,gpr->kgr", forward, grouped, precision=highest, preferred_element_type=jnp.float32
    )
    share = lax.psum_scatter(
        out.reshape(share_rows * lax.axis_size("phi"), groups * rows_here),
        "phi",
        scatter_dimension=0,
        tiled=True,
    )
    share_index = phi_index * share_rows + jnp.arange(share_rows, dtype=jnp.int32)
    keep = (share_index % KMAX)[:, None] < line_counts[None, :]
    masked = jnp.where(keep, share, 0.0)
    piece = lax.all_gather(masked, "phi", axis=0, tiled=True)
    stacked = piece.reshape(piece.shape[0], groups, rows_here)
    result = jnp.einsum(
        "kp,kgr->gpr", backward, stacked, precision=highest, preferred_element_type=jnp.float32
    )
    return result.reshape(lines.shape)


def halves(x):
    high = x.astype(jnp.bfloat16)
    return high, (x - high.astype(jnp.float32)).astype(jnp.bfloat16)


def host_halves(x):
    x = x.astype(np.float32)
    high = x.astype(ml_dtypes.bfloat16)
    return high, (x - high.astype(np.float32)).astype(ml_dtypes.bfloat16)


def host_tables(half):
    points = 2 * half
    azimuth = np.arange(half)
    mode = np.arange(KMAX)
    angle = (mode[:, None] * azimuth[None, :] % points) * (2.0 * math.pi / points)
    cos, sin = np.cos(angle), np.sin(angle)
    weight = (np.where(mode == 0, 1.0, 2.0) / points)[:, None]
    up = np.concatenate([cos, sin])
    down = np.concatenate([cos[::-1], sin[::-1]])
    up_back = np.concatenate([cos * weight, sin * weight]).T
    down_back = np.concatenate([(cos * weight)[::-1], (sin * weight)[::-1]]).T
    return [part for t in (up, down, up_back, down_back) for part in host_halves(t)]


def order_kernel(all_ref, own_ref, spread_ref, gather_ref, kept_ref, longest_ref):
    half = LANES // 2

    def sort(counts):
        across = jnp.broadcast_to(counts, (LANES, LANES))
        down = across.T
        lane = lax.broadcasted_iota(jnp.int32, (LANES, LANES), 1)
        line = lax.broadcasted_iota(jnp.int32, (LANES, LANES), 0)
        ahead = jnp.where((across > down) | ((across == down) & (lane < line)), 1.0, 0.0)
        behind = jnp.where((down > across) | ((across == down) & (line < lane)), 1.0, 0.0)
        rank_down = jnp.sum(ahead, axis=1, keepdims=True)
        rank_across = jnp.sum(behind, axis=0, keepdims=True)
        place = lambda r: jnp.where(r < half, r, 2.0 * LANES - 1.0 - r)
        to_down = jnp.concatenate([place(rank_down), place(rank_down) + half], axis=0)
        to_across = jnp.concatenate([place(rank_across), place(rank_across) + half], axis=1)
        lane2 = lax.broadcasted_iota(jnp.int32, (2 * LANES, 2 * LANES), 1).astype(jnp.float32)
        line2 = lax.broadcasted_iota(jnp.int32, (2 * LANES, 2 * LANES), 0).astype(jnp.float32)
        spread = jnp.where(lane2 == to_down, 1.0, 0.0)
        gather = jnp.where(line2 == to_across, 1.0, 0.0)
        counts_down = jnp.concatenate([down[:, :1], down[:, :1]], axis=0)
        kept = jnp.sum(spread * counts_down, axis=0, keepdims=True)
        return spread, gather, kept

    spread, gather, kept = sort(own_ref[...].astype(jnp.float32))
    spread_ref[...] = spread.astype(jnp.bfloat16)
    gather_ref[...] = gather.astype(jnp.bfloat16)
    kept_ref[...] = kept.astype(jnp.int32)
    longest = jnp.zeros((1, LANES), jnp.float32)
    for band in range(all_ref.shape[0]):
        _, _, kept = sort(all_ref[band : band + 1, :].astype(jnp.float32))
        longest = jnp.maximum(longest, kept[:, :LANES] + kept[:, LANES:])
    longest_ref[0] = jnp.max(longest).astype(jnp.int32)


def exchange_kernel(
    length,
    x_hbm,
    *refs,
):
    table_hbm = refs[:8]
    spread_ref, gather_ref, kept_ref, out_hbm = refs[8:12]
    table = refs[12:20]
    x_ref, send_ref, recv_ref, sign_ref, large, small, c_large, c_small = refs[20:28]
    table_sem, in_sem, out_sem, send_sem, recv_sem = refs[28:]
    steps = x_ref.shape[0]
    points = x_ref.shape[2]
    start_small = length - KMAX
    other = 1 - lax.axis_index("phi")

    def copy_in(s):
        return pltpu.make_async_copy(x_hbm.at[pl.ds(2 * s, 2)], x_ref.at[s], in_sem.at[s])

    def copy_out(s):
        return pltpu.make_async_copy(x_ref.at[s], out_hbm.at[pl.ds(2 * s, 2)], out_sem.at[s])

    def copy_table(i):
        return pltpu.make_async_copy(table_hbm[i], table[i], table_sem.at[i])

    def exchange(s):
        return pltpu.make_async_remote_copy(
            src_ref=send_ref.at[s],
            dst_ref=recv_ref.at[s],
            send_sem=send_sem.at[s],
            recv_sem=recv_sem.at[s],
            device_id={"phi": other},
            device_id_type=pl.DeviceIdType.MESH,
        )

    copy_in(0).start()
    for i in range(4):
        copy_table(i).start()
    barrier = pltpu.get_barrier_semaphore()
    pl.semaphore_signal(
        barrier, inc=1, device_id={"phi": other}, device_id_type=pl.DeviceIdType.MESH
    )

    @pl.loop(1, steps)
    def _(s):
        copy_in(s).start()

    for i in range(4, 8):
        copy_table(i).start()

    kept_large = kept_ref[:, :LANES]
    kept_small = kept_ref[:, LANES:]
    row = lax.broadcasted_iota(jnp.int32, (length, LANES), 0)
    parity = jnp.where(row < kept_large, row, length - 1 - row) % 2
    sign_ref[...] = 1.0 - 2.0 * parity.astype(jnp.float32)
    mode = lax.broadcasted_iota(jnp.int32, (KMAX, LANES), 0)

    def dot(a, b):
        return jnp.dot(a, b, preferred_element_type=jnp.float32)

    def product(high_ref, low_ref, rows, operand):
        wide = dot(high_ref[rows, :], operand[...])
        return wide[:, :LANES] + wide[:, LANES:] + dot(low_ref[rows, :], operand[:, :LANES])

    for i in range(4):
        copy_table(i).wait()
    pl.semaphore_wait(barrier, 1)

    @pl.loop(0, steps)
    def _(s):
        copy_in(s).wait()

        @pl.loop(0, points // TILE)
        def _(t):
            rows = pl.ds(pl.multiple_of(t * TILE, TILE), TILE)
            both = jnp.concatenate([x_ref[s, 0, rows, :], x_ref[s, 1, rows, :]], axis=1)
            high, low = halves(both)
            high = dot(high, spread_ref[...]).astype(jnp.bfloat16)
            low = dot(low, spread_ref[...]).astype(jnp.bfloat16)
            large[rows, :] = jnp.concatenate([high[:, :LANES], low[:, :LANES]], axis=1)
            small[rows, :] = jnp.concatenate([high[:, LANES:], low[:, LANES:]], axis=1)

        @pl.loop(0, 2 * KMAX // TILE)
        def _(t):
            rows = pl.ds(pl.multiple_of(t * TILE, TILE), TILE)
            c_large[rows, :] = product(table[0], table[1], rows, large)
            c_small[rows, :] = product(table[2], table[3], rows, small)

        for part in range(2):
            rows = pl.ds(part * KMAX, KMAX)
            down = jnp.where(KMAX - 1 - mode < kept_small, c_small[rows, :], 0.0)
            up = jnp.where(mode < kept_large, c_large[rows, :], 0.0)
            send_ref[s, part, pl.ds(0, KMAX), :] = up
            if start_small < KMAX:
                shared = KMAX - start_small
                send_ref[s, part, pl.ds(start_small, shared), :] = up[start_small:] + down[:shared]
            if start_small > 0:
                send_ref[s, part, pl.ds(KMAX, start_small), :] = down[KMAX - start_small :]
        exchange(s).start()

    for i in range(4, 8):
        copy_table(i).wait()

    @pl.loop(0, steps)
    def _(s):
        exchange(s).wait_recv()
        for part in range(2):
            rows = pl.ds(part * KMAX, KMAX)
            total = send_ref[s, part] + sign_ref[...] * recv_ref[s, part]
            up = jnp.where(mode < kept_large, total[:KMAX], 0.0)
            down = jnp.where(KMAX - 1 - mode < kept_small, total[start_small:], 0.0)
            large[rows, :] = jnp.concatenate(halves(up), axis=1)
            small[rows, :] = jnp.concatenate(halves(down), axis=1)

        @pl.loop(0, points // TILE)
        def _(t):
            rows = pl.ds(pl.multiple_of(t * TILE, TILE), TILE)
            result = jnp.concatenate(
                [
                    product(table[4], table[5], rows, large),
                    product(table[6], table[7], rows, small),
                ],
                axis=1,
            )
            high, low = halves(result)
            result = dot(high, gather_ref[...]) + dot(low, gather_ref[...])
            x_ref[s, 0, rows, :] = result[:, :LANES]
            x_ref[s, 1, rows, :] = result[:, LANES:]

        copy_out(s).start()

    @pl.loop(0, steps)
    def _(s):
        exchange(s).wait_send()
        copy_out(s).wait()


def exchange(length, collective_id, lines, host, spread, gather, kept):
    groups, points, lanes = lines.shape
    steps = groups // 2
    anywhere = pl.BlockSpec(memory_space=pl.ANY)
    inside = pl.BlockSpec(memory_space=pltpu.VMEM)
    dma = pltpu.SemaphoreType.DMA
    deep = max(points, 2 * KMAX)
    return pl.pallas_call(
        functools.partial(exchange_kernel, length),
        out_shape=jax.ShapeDtypeStruct(lines.shape, jnp.float32),
        in_specs=[anywhere] * 9 + [inside] * 3,
        out_specs=anywhere,
        scratch_shapes=[pltpu.VMEM(t.shape, jnp.bfloat16) for t in host]
        + [
            pltpu.VMEM((steps, 2, points, lanes), jnp.float32),
            pltpu.VMEM((steps, 2, length, lanes), jnp.float32),
            pltpu.VMEM((steps, 2, length, lanes), jnp.float32),
            pltpu.VMEM((length, lanes), jnp.float32),
            pltpu.VMEM((deep, 2 * lanes), jnp.bfloat16),
            pltpu.VMEM((deep, 2 * lanes), jnp.bfloat16),
            pltpu.VMEM((2 * KMAX, lanes), jnp.float32),
            pltpu.VMEM((2 * KMAX, lanes), jnp.float32),
            dma((8,)),
            dma((steps,)),
            dma((steps,)),
            dma((steps,)),
            dma((steps,)),
        ],
        compiler_params=pltpu.CompilerParams(
            collective_id=collective_id,
            has_side_effects=True,
            vmem_limit_bytes=56 * 1024 * 1024,
        ),
        name="exchange_" + str(length),
    )(lines, *host, spread, gather, kept)


LENGTHS = (400, 416, 432, 448, 480, 576, 2 * KMAX)


def paired(lines, count_table, row_counts):
    nfields, shells, points, lanes = lines.shape
    whole = pl.BlockSpec(memory_space=pltpu.VMEM)
    spread, gather, kept, longest = pl.pallas_call(
        order_kernel,
        out_shape=(
            jax.ShapeDtypeStruct((2 * lanes, 2 * lanes), jnp.bfloat16),
            jax.ShapeDtypeStruct((2 * lanes, 2 * lanes), jnp.bfloat16),
            jax.ShapeDtypeStruct((1, 2 * lanes), jnp.int32),
            jax.ShapeDtypeStruct((1,), jnp.int32),
        ),
        in_specs=[whole, whole],
        out_specs=(whole, whole, whole, pl.BlockSpec(memory_space=pltpu.SMEM)),
        name="order_rows",
    )(count_table, row_counts[None, :])
    host = [jnp.asarray(t) for t in host_tables(points)]
    branch = jnp.sum((longest[0] > jnp.asarray(LENGTHS[:-1], jnp.int32)).astype(jnp.int32))
    branches = [
        functools.partial(exchange, length, index) for index, length in enumerate(LENGTHS)
    ]
    grouped = lines.reshape(nfields * shells, points, lanes)
    result = lax.switch(branch, branches, grouped, host, spread, gather, kept)
    return result.reshape(lines.shape)


def on_device(fields, kept_counts):
    n_theta = lax.axis_size("theta")
    theta_index = lax.axis_index("theta")
    band_rows = fields.shape[3]
    caps = kept_counts.shape[0] // band_rows
    cap_bands = caps // 2
    count_table = kept_counts.reshape(caps, band_rows)
    low_side = theta_index < cap_bands
    high_side = theta_index >= n_theta - cap_bands
    position = jnp.where(low_side, theta_index, theta_index - (n_theta - 2 * cap_bands))
    position = jnp.clip(position, 0, caps - 1)
    row_counts = lax.dynamic_index_in_dim(count_table, position, 0, keepdims=False)
    fits = (
        lax.axis_size("phi") == 2
        and band_rows == LANES
        and fields.shape[0] * fields.shape[1] % 2 == 0
        and fields.shape[2] % TILE == 0
    )
    if fits:
        smoothed = paired(fields, count_table, row_counts)
    else:
        smoothed = spectral(fields, row_counts)
    if n_theta == caps:
        return smoothed
    return jnp.where(jnp.logical_or(low_side, high_side), smoothed, fields)


def solution(mesh):
    placed = (P(None, "row", "phi", "theta"), P())
    return jax.shard_map(
        on_device,
        mesh=mesh,
        in_specs=placed,
        out_specs=P(None, "row", "phi", "theta"),
        check_vma=False,
    )
```

```python
import functools
import math

import jax
import jax.numpy as jnp
import ml_dtypes
import numpy as np
from jax import lax
from jax.experimental import pallas as pl
from jax.experimental.pallas import tpu as pltpu
from jax.sharding import PartitionSpec as P

KMAX = 384
TILE = 128
LANES = 128
LENGTHS = tuple(range(KMAX, 472, 8)) + (480, 496, 528, 576, 2 * KMAX)


def tables(offset, span_rows, points, mode_count):
    azimuth = offset + jnp.arange(span_rows, dtype=jnp.int32)
    wavenumber = jnp.arange(mode_count, dtype=jnp.int32)
    phase_turns = azimuth[:, None] * wavenumber[None, :] % points
    angles = phase_turns.astype(jnp.float32) * (2.0 * math.pi / points)
    forward = jnp.concatenate([jnp.cos(angles), jnp.sin(angles)], axis=1)
    weight = jnp.where(wavenumber == 0, 1.0, 2.0).astype(jnp.float32) / points
    weight = jnp.concatenate([weight, weight])
    backward = (forward * weight[None, :]).T
    return (forward, backward)


def spectral(lines, row_counts):
    nfields, shells, local_points, rows_here = lines.shape
    n_phi = lax.axis_size("phi")
    points = local_points * n_phi
    highest = lax.Precision.HIGHEST
    groups = nfields * shells
    grouped = lines.reshape(groups, local_points, rows_here)
    line_counts = jnp.broadcast_to(row_counts[None, :], (groups, rows_here)).reshape(-1)
    phi_index = lax.axis_index("phi")
    forward, backward = tables(phi_index * local_points, local_points, points, KMAX)
    share_rows = forward.shape[1] // n_phi
    out = jnp.einsum(
        "pk,gpr->kgr", forward, grouped, precision=highest, preferred_element_type=jnp.float32
    )
    share = lax.psum_scatter(
        out.reshape(share_rows * lax.axis_size("phi"), groups * rows_here),
        "phi",
        scatter_dimension=0,
        tiled=True,
    )
    share_index = phi_index * share_rows + jnp.arange(share_rows, dtype=jnp.int32)
    keep = (share_index % KMAX)[:, None] < line_counts[None, :]
    masked = jnp.where(keep, share, 0.0)
    piece = lax.all_gather(masked, "phi", axis=0, tiled=True)
    stacked = piece.reshape(piece.shape[0], groups, rows_here)
    result = jnp.einsum(
        "kp,kgr->gpr", backward, stacked, precision=highest, preferred_element_type=jnp.float32
    )
    return result.reshape(lines.shape)


def halves(x):
    high = x.astype(jnp.bfloat16)
    return high, (x - high.astype(jnp.float32)).astype(jnp.bfloat16)


def host_halves(x):
    x = x.astype(np.float32)
    high = x.astype(ml_dtypes.bfloat16)
    return high, (x - high.astype(np.float32)).astype(ml_dtypes.bfloat16)


def host_tables(half):
    points = 2 * half
    azimuth = np.arange(half)
    mode = np.arange(KMAX)
    angle = (mode[:, None] * azimuth[None, :] % points) * (2.0 * math.pi / points)
    cos, sin = np.cos(angle), np.sin(angle)
    weight = (np.where(mode == 0, 1.0, 2.0) / points)[:, None]
    up = np.concatenate([cos, sin])
    down = np.concatenate([cos[::-1], sin[::-1]])
    up_back = np.concatenate([cos * weight, sin * weight]).T
    down_back = np.concatenate([(cos * weight)[::-1], (sin * weight)[::-1]]).T
    return [part for t in (up, down, up_back, down_back) for part in host_halves(t)]


def order_kernel(all_ref, spread_ref, gather_ref, kept_ref, branch_ref):
    half = LANES // 2

    def sort(counts):
        across = jnp.broadcast_to(counts, (LANES, LANES))
        down = across.T
        lane = lax.broadcasted_iota(jnp.int32, (LANES, LANES), 1)
        line = lax.broadcasted_iota(jnp.int32, (LANES, LANES), 0)
        ahead = jnp.where((across > down) | ((across == down) & (lane < line)), 1.0, 0.0)
        behind = jnp.where((down > across) | ((across == down) & (line < lane)), 1.0, 0.0)
        rank_down = jnp.sum(ahead, axis=1, keepdims=True)
        rank_across = jnp.sum(behind, axis=0, keepdims=True)
        place = lambda r: jnp.where(r < half, r, 2.0 * LANES - 1.0 - r)
        to_down = jnp.concatenate([place(rank_down), place(rank_down) + half], axis=0)
        to_across = jnp.concatenate([place(rank_across), place(rank_across) + half], axis=1)
        lane2 = lax.broadcasted_iota(jnp.int32, (2 * LANES, 2 * LANES), 1).astype(jnp.float32)
        line2 = lax.broadcasted_iota(jnp.int32, (2 * LANES, 2 * LANES), 0).astype(jnp.float32)
        spread = jnp.where(lane2 == to_down, 1.0, 0.0)
        gather = jnp.where(line2 == to_across, 1.0, 0.0)
        counts_down = jnp.concatenate([down[:, :1], down[:, :1]], axis=0)
        kept = jnp.sum(spread * counts_down, axis=0, keepdims=True)
        return spread, gather, kept

    bands = all_ref.shape[0]
    n_theta = lax.axis_size("theta")
    theta_index = lax.axis_index("theta")
    position = jnp.where(
        theta_index < bands // 2, theta_index, theta_index - (n_theta - bands // 2 * 2)
    )
    position = jnp.clip(position, 0, bands - 1)
    own = all_ref[0:1, :]
    for band in range(1, bands):
        own = jnp.where(position == band, all_ref[band : band + 1, :], own)
    spread, gather, kept = sort(own.astype(jnp.float32))
    spread_ref[...] = spread.astype(jnp.bfloat16)
    gather_ref[...] = gather.astype(jnp.bfloat16)
    kept_ref[...] = kept.astype(jnp.int32)
    longest = jnp.zeros((1, LANES), jnp.float32)
    for band in range(bands):
        _, _, kept = sort(all_ref[band : band + 1, :].astype(jnp.float32))
        longest = jnp.maximum(longest, kept[:, :LANES] + kept[:, LANES:])
    longest = jnp.max(longest).astype(jnp.int32)
    branch = jnp.int32(0)
    for length in LENGTHS[:-1]:
        branch += (longest > length).astype(jnp.int32)
    branch_ref[0] = branch


def exchange_kernel(
    length,
    x_hbm,
    *refs,
):
    table_hbm = refs[:8]
    spread_ref, gather_ref, kept_ref, out_hbm = refs[8:12]
    table = refs[12:20]
    x_ref, send_ref, recv_ref, sign_ref, large, small, c_large, c_small = refs[20:28]
    table_sem, in_sem, out_sem, send_sem, recv_sem = refs[28:]
    steps = x_ref.shape[0]
    points = x_ref.shape[2]
    start_small = length - KMAX
    other = 1 - lax.axis_index("phi")

    def copy_in(s):
        return pltpu.make_async_copy(x_hbm.at[pl.ds(2 * s, 2)], x_ref.at[s], in_sem.at[s])

    def copy_out(s):
        return pltpu.make_async_copy(x_ref.at[s], out_hbm.at[pl.ds(2 * s, 2)], out_sem.at[s])

    def copy_table(i):
        return pltpu.make_async_copy(table_hbm[i], table[i], table_sem.at[i])

    def exchange(s):
        return pltpu.make_async_remote_copy(
            src_ref=send_ref.at[s],
            dst_ref=recv_ref.at[s],
            send_sem=send_sem.at[s],
            recv_sem=recv_sem.at[s],
            device_id={"phi": other},
            device_id_type=pl.DeviceIdType.MESH,
        )

    copy_in(0).start()
    for i in range(4):
        copy_table(i).start()
    barrier = pltpu.get_barrier_semaphore()
    pl.semaphore_signal(
        barrier, inc=1, device_id={"phi": other}, device_id_type=pl.DeviceIdType.MESH
    )

    @pl.loop(1, steps)
    def _(s):
        copy_in(s).start()

    for i in range(4, 8):
        copy_table(i).start()

    kept_large = kept_ref[:, :LANES]
    kept_small = kept_ref[:, LANES:]
    row = lax.broadcasted_iota(jnp.int32, (length, LANES), 0)
    parity = jnp.where(row < kept_large, row, length - 1 - row) % 2
    sign_ref[...] = 1.0 - 2.0 * parity.astype(jnp.float32)
    mode = lax.broadcasted_iota(jnp.int32, (KMAX, LANES), 0)

    def dot(a, b):
        return jnp.dot(a, b, preferred_element_type=jnp.float32)

    def product(high_ref, low_ref, rows, operand):
        wide = dot(high_ref[rows, :], operand[...])
        return wide[:, :LANES] + wide[:, LANES:] + dot(low_ref[rows, :], operand[:, :LANES])

    for i in range(4):
        copy_table(i).wait()
    pl.semaphore_wait(barrier, 1)

    @pl.loop(0, steps)
    def _(s):
        copy_in(s).wait()

        @pl.loop(0, points // TILE)
        def _(t):
            rows = pl.ds(pl.multiple_of(t * TILE, TILE), TILE)
            both = jnp.concatenate([x_ref[s, 0, rows, :], x_ref[s, 1, rows, :]], axis=1)
            high, low = halves(both)
            high = dot(high, spread_ref[...]).astype(jnp.bfloat16)
            low = dot(low, spread_ref[...]).astype(jnp.bfloat16)
            large[rows, :] = jnp.concatenate([high[:, :LANES], low[:, :LANES]], axis=1)
            small[rows, :] = jnp.concatenate([high[:, LANES:], low[:, LANES:]], axis=1)

        @pl.loop(0, 2 * KMAX // TILE)
        def _(t):
            rows = pl.ds(pl.multiple_of(t * TILE, TILE), TILE)
            c_large[rows, :] = product(table[0], table[1], rows, large)
            c_small[rows, :] = product(table[2], table[3], rows, small)

        for part in range(2):
            rows = pl.ds(part * KMAX, KMAX)
            down = jnp.where(KMAX - 1 - mode < kept_small, c_small[rows, :], 0.0)
            up = jnp.where(mode < kept_large, c_large[rows, :], 0.0)
            send_ref[s, part, pl.ds(0, KMAX), :] = up
            if start_small < KMAX:
                shared = KMAX - start_small
                send_ref[s, part, pl.ds(start_small, shared), :] = up[start_small:] + down[:shared]
            if start_small > 0:
                send_ref[s, part, pl.ds(KMAX, start_small), :] = down[KMAX - start_small :]
        exchange(s).start()

    for i in range(4, 8):
        copy_table(i).wait()

    @pl.loop(0, steps)
    def _(s):
        exchange(s).wait_recv()
        for part in range(2):
            rows = pl.ds(part * KMAX, KMAX)
            total = send_ref[s, part] + sign_ref[...] * recv_ref[s, part]
            up = jnp.where(mode < kept_large, total[:KMAX], 0.0)
            down = jnp.where(KMAX - 1 - mode < kept_small, total[start_small:], 0.0)
            large[rows, :] = jnp.concatenate(halves(up), axis=1)
            small[rows, :] = jnp.concatenate(halves(down), axis=1)

        @pl.loop(0, points // TILE)
        def _(t):
            rows = pl.ds(pl.multiple_of(t * TILE, TILE), TILE)
            result = jnp.concatenate(
                [
                    product(table[4], table[5], rows, large),
                    product(table[6], table[7], rows, small),
                ],
                axis=1,
            )
            high, low = halves(result)
            result = dot(high, gather_ref[...]) + dot(low, gather_ref[...])
            x_ref[s, 0, rows, :] = result[:, :LANES]
            x_ref[s, 1, rows, :] = result[:, LANES:]

        copy_out(s).start()

    @pl.loop(0, steps)
    def _(s):
        exchange(s).wait_send()
        copy_out(s).wait()


def exchange(length, collective_id, lines, host, spread, gather, kept):
    groups, points, lanes = lines.shape
    steps = groups // 2
    anywhere = pl.BlockSpec(memory_space=pl.ANY)
    inside = pl.BlockSpec(memory_space=pltpu.VMEM)
    dma = pltpu.SemaphoreType.DMA
    deep = max(points, 2 * KMAX)
    return pl.pallas_call(
        functools.partial(exchange_kernel, length),
        out_shape=jax.ShapeDtypeStruct(lines.shape, jnp.float32),
        in_specs=[anywhere] * 9 + [inside] * 3,
        out_specs=anywhere,
        scratch_shapes=[pltpu.VMEM(t.shape, jnp.bfloat16) for t in host]
        + [
            pltpu.VMEM((steps, 2, points, lanes), jnp.float32),
            pltpu.VMEM((steps, 2, length, lanes), jnp.float32),
            pltpu.VMEM((steps, 2, length, lanes), jnp.float32),
            pltpu.VMEM((length, lanes), jnp.float32),
            pltpu.VMEM((deep, 2 * lanes), jnp.bfloat16),
            pltpu.VMEM((deep, 2 * lanes), jnp.bfloat16),
            pltpu.VMEM((2 * KMAX, lanes), jnp.float32),
            pltpu.VMEM((2 * KMAX, lanes), jnp.float32),
            dma((8,)),
            dma((steps,)),
            dma((steps,)),
            dma((steps,)),
            dma((steps,)),
        ],
        compiler_params=pltpu.CompilerParams(
            collective_id=collective_id,
            has_side_effects=True,
            vmem_limit_bytes=56 * 1024 * 1024,
        ),
        name="exchange_" + str(length),
    )(lines, *host, spread, gather, kept)


def paired(lines, count_table):
    nfields, shells, points, lanes = lines.shape
    whole = pl.BlockSpec(memory_space=pltpu.VMEM)
    spread, gather, kept, branch = pl.pallas_call(
        order_kernel,
        out_shape=(
            jax.ShapeDtypeStruct((2 * lanes, 2 * lanes), jnp.bfloat16),
            jax.ShapeDtypeStruct((2 * lanes, 2 * lanes), jnp.bfloat16),
            jax.ShapeDtypeStruct((1, 2 * lanes), jnp.int32),
            jax.ShapeDtypeStruct((1,), jnp.int32),
        ),
        in_specs=[whole],
        out_specs=(whole, whole, whole, pl.BlockSpec(memory_space=pltpu.SMEM)),
        name="order_rows",
    )(count_table)
    host = [jnp.asarray(t) for t in host_tables(points)]
    branches = [
        functools.partial(exchange, length, index) for index, length in enumerate(LENGTHS)
    ]
    grouped = lines.reshape(nfields * shells, points, lanes)
    result = lax.switch(branch[0], branches, grouped, host, spread, gather, kept)
    return result.reshape(lines.shape)


def on_device(fields, kept_counts):
    n_theta = lax.axis_size("theta")
    theta_index = lax.axis_index("theta")
    band_rows = fields.shape[3]
    caps = kept_counts.shape[0] // band_rows
    cap_bands = caps // 2
    count_table = kept_counts.reshape(caps, band_rows)
    low_side = theta_index < cap_bands
    high_side = theta_index >= n_theta - cap_bands
    position = jnp.where(low_side, theta_index, theta_index - (n_theta - 2 * cap_bands))
    position = jnp.clip(position, 0, caps - 1)
    row_counts = lax.dynamic_index_in_dim(count_table, position, 0, keepdims=False)
    fits = (
        lax.axis_size("phi") == 2
        and band_rows == LANES
        and fields.shape[0] * fields.shape[1] % 2 == 0
        and fields.shape[2] % TILE == 0
    )
    if fits:
        smoothed = paired(fields, count_table)
    else:
        smoothed = spectral(fields, row_counts)
    if n_theta == caps:
        return smoothed
    return jnp.where(jnp.logical_or(low_side, high_side), smoothed, fields)


def solution(mesh):
    placed = (P(None, "row", "phi", "theta"), P())
    return jax.shard_map(
        on_device,
        mesh=mesh,
        in_specs=placed,
        out_specs=P(None, "row", "phi", "theta"),
        check_vma=False,
    )
```

```python
import functools
import math

import jax
import jax.numpy as jnp
import numpy as np
from jax import lax
from jax.experimental import pallas as pl
from jax.experimental.pallas import tpu as pltpu
from jax.sharding import PartitionSpec as P

KMAX = 384
TILE = 128
LANES = 128
LENGTHS = tuple(range(KMAX, 472, 8)) + (480, 496, 528, 576, 2 * KMAX)


def tables(offset, span_rows, points, mode_count):
    azimuth = offset + jnp.arange(span_rows, dtype=jnp.int32)
    wavenumber = jnp.arange(mode_count, dtype=jnp.int32)
    phase_turns = azimuth[:, None] * wavenumber[None, :] % points
    angles = phase_turns.astype(jnp.float32) * (2.0 * math.pi / points)
    forward = jnp.concatenate([jnp.cos(angles), jnp.sin(angles)], axis=1)
    weight = jnp.where(wavenumber == 0, 1.0, 2.0).astype(jnp.float32) / points
    weight = jnp.concatenate([weight, weight])
    backward = (forward * weight[None, :]).T
    return (forward, backward)


def spectral(lines, row_counts):
    nfields, shells, local_points, rows_here = lines.shape
    n_phi = lax.axis_size("phi")
    points = local_points * n_phi
    highest = lax.Precision.HIGHEST
    groups = nfields * shells
    grouped = lines.reshape(groups, local_points, rows_here)
    line_counts = jnp.broadcast_to(row_counts[None, :], (groups, rows_here)).reshape(-1)
    phi_index = lax.axis_index("phi")
    forward, backward = tables(phi_index * local_points, local_points, points, KMAX)
    share_rows = forward.shape[1] // n_phi
    out = jnp.einsum(
        "pk,gpr->kgr", forward, grouped, precision=highest, preferred_element_type=jnp.float32
    )
    share = lax.psum_scatter(
        out.reshape(share_rows * lax.axis_size("phi"), groups * rows_here),
        "phi",
        scatter_dimension=0,
        tiled=True,
    )
    share_index = phi_index * share_rows + jnp.arange(share_rows, dtype=jnp.int32)
    keep = (share_index % KMAX)[:, None] < line_counts[None, :]
    masked = jnp.where(keep, share, 0.0)
    piece = lax.all_gather(masked, "phi", axis=0, tiled=True)
    stacked = piece.reshape(piece.shape[0], groups, rows_here)
    result = jnp.einsum(
        "kp,kgr->gpr", backward, stacked, precision=highest, preferred_element_type=jnp.float32
    )
    return result.reshape(lines.shape)


def halves(x):
    high = x.astype(jnp.bfloat16)
    return high, (x - high.astype(jnp.float32)).astype(jnp.bfloat16)


def host_tables(half):
    points = 2 * half
    azimuth = np.arange(half)
    mode = np.arange(KMAX)
    angle = (mode[:, None] * azimuth[None, :] % points) * (2.0 * math.pi / points)
    cos, sin = np.cos(angle), np.sin(angle)
    weight = (np.where(mode == 0, 1.0, 2.0) / points)[:, None]
    up = np.concatenate([cos, sin])
    down = np.concatenate([cos[::-1], sin[::-1]])
    up_back = np.concatenate([cos * weight, sin * weight]).T
    down_back = np.concatenate([(cos * weight)[::-1], (sin * weight)[::-1]]).T
    return [t.astype(np.float32) for t in (up, down, up_back, down_back)]


def order_kernel(all_ref, spread_ref, gather_ref, kept_ref, branch_ref):
    half = LANES // 2

    def sort(counts):
        across = jnp.broadcast_to(counts, (LANES, LANES))
        down = across.T
        lane = lax.broadcasted_iota(jnp.int32, (LANES, LANES), 1)
        line = lax.broadcasted_iota(jnp.int32, (LANES, LANES), 0)
        ahead = jnp.where((across > down) | ((across == down) & (lane < line)), 1.0, 0.0)
        behind = jnp.where((down > across) | ((across == down) & (line < lane)), 1.0, 0.0)
        rank_down = jnp.sum(ahead, axis=1, keepdims=True)
        rank_across = jnp.sum(behind, axis=0, keepdims=True)
        place = lambda r: jnp.where(r < half, r, 2.0 * LANES - 1.0 - r)
        to_down = jnp.concatenate([place(rank_down), place(rank_down) + half], axis=0)
        to_across = jnp.concatenate([place(rank_across), place(rank_across) + half], axis=1)
        lane2 = lax.broadcasted_iota(jnp.int32, (2 * LANES, 2 * LANES), 1).astype(jnp.float32)
        line2 = lax.broadcasted_iota(jnp.int32, (2 * LANES, 2 * LANES), 0).astype(jnp.float32)
        spread = jnp.where(lane2 == to_down, 1.0, 0.0)
        gather = jnp.where(line2 == to_across, 1.0, 0.0)
        counts_down = jnp.concatenate([down[:, :1], down[:, :1]], axis=0)
        kept = jnp.sum(spread * counts_down, axis=0, keepdims=True)
        return spread, gather, kept

    bands = all_ref.shape[0]
    n_theta = lax.axis_size("theta")
    theta_index = lax.axis_index("theta")
    position = jnp.where(
        theta_index < bands // 2, theta_index, theta_index - (n_theta - bands // 2 * 2)
    )
    position = jnp.clip(position, 0, bands - 1)
    own = all_ref[0:1, :]
    for band in range(1, bands):
        own = jnp.where(position == band, all_ref[band : band + 1, :], own)
    spread, gather, kept = sort(own.astype(jnp.float32))
    spread_ref[...] = spread.astype(jnp.bfloat16)
    gather_ref[...] = gather.astype(jnp.bfloat16)
    kept_ref[...] = kept.astype(jnp.int32)
    longest = jnp.zeros((1, LANES), jnp.float32)
    for band in range(bands):
        _, _, kept = sort(all_ref[band : band + 1, :].astype(jnp.float32))
        longest = jnp.maximum(longest, kept[:, :LANES] + kept[:, LANES:])
    longest = jnp.max(longest).astype(jnp.int32)
    branch = jnp.int32(0)
    for length in LENGTHS[:-1]:
        branch += (longest > length).astype(jnp.int32)
    branch_ref[0] = branch


def exchange_kernel(
    length,
    x_hbm,
    *refs,
):
    table_hbm = refs[:4]
    spread_ref, gather_ref, kept_ref, x_ref = refs[4:8]
    staged, table = refs[8:12], refs[12:20]
    send_ref, recv_ref, sign_ref, large, small, c_large, c_small = refs[20:27]
    table_sem, in_sem, send_sem, recv_sem = refs[27:]
    steps = x_ref.shape[0] // 2
    points = x_ref.shape[1]
    start_small = length - KMAX
    other = 1 - lax.axis_index("phi")

    def copy_in(s):
        pair = pl.ds(2 * s, 2)
        return pltpu.make_async_copy(x_hbm.at[pair], x_ref.at[pair], in_sem.at[s])

    def copy_table(i):
        return pltpu.make_async_copy(table_hbm[i], staged[i], table_sem.at[i])

    def split_table(i):
        copy_table(i).wait()

        @pl.loop(0, staged[i].shape[0] // TILE)
        def _(t):
            rows = pl.ds(pl.multiple_of(t * TILE, TILE), TILE)
            high, low = halves(staged[i][rows, :])
            table[2 * i][rows, :] = high
            table[2 * i + 1][rows, :] = low

    def exchange(s):
        return pltpu.make_async_remote_copy(
            src_ref=send_ref.at[s],
            dst_ref=recv_ref.at[s],
            send_sem=send_sem.at[s],
            recv_sem=recv_sem.at[s],
            device_id={"phi": other},
            device_id_type=pl.DeviceIdType.MESH,
        )

    copy_in(0).start()
    for i in range(2):
        copy_table(i).start()
    barrier = pltpu.get_barrier_semaphore()
    pl.semaphore_signal(
        barrier, inc=1, device_id={"phi": other}, device_id_type=pl.DeviceIdType.MESH
    )

    @pl.loop(1, steps)
    def _(s):
        copy_in(s).start()

    for i in range(2, 4):
        copy_table(i).start()

    kept_large = kept_ref[:, :LANES]
    kept_small = kept_ref[:, LANES:]
    row = lax.broadcasted_iota(jnp.int32, (length, LANES), 0)
    parity = jnp.where(row < kept_large, row, length - 1 - row) % 2
    sign_ref[...] = 1.0 - 2.0 * parity.astype(jnp.float32)
    mode = lax.broadcasted_iota(jnp.int32, (KMAX, LANES), 0)

    def dot(a, b):
        return jnp.dot(a, b, preferred_element_type=jnp.float32)

    def product(high_ref, low_ref, rows, operand):
        wide = dot(high_ref[rows, :], operand[...])
        return wide[:, :LANES] + wide[:, LANES:] + dot(low_ref[rows, :], operand[:, :LANES])

    for i in range(2):
        split_table(i)
    pl.semaphore_wait(barrier, 1)

    @pl.loop(0, steps)
    def _(s):
        copy_in(s).wait()

        @pl.loop(0, points // TILE)
        def _(t):
            rows = pl.ds(pl.multiple_of(t * TILE, TILE), TILE)
            both = jnp.concatenate([x_ref[2 * s, rows, :], x_ref[2 * s + 1, rows, :]], axis=1)
            high, low = halves(both)
            high = dot(high, spread_ref[...]).astype(jnp.bfloat16)
            low = dot(low, spread_ref[...]).astype(jnp.bfloat16)
            large[rows, :] = jnp.concatenate([high[:, :LANES], low[:, :LANES]], axis=1)
            small[rows, :] = jnp.concatenate([high[:, LANES:], low[:, LANES:]], axis=1)

        @pl.loop(0, 2 * KMAX // TILE)
        def _(t):
            rows = pl.ds(pl.multiple_of(t * TILE, TILE), TILE)
            c_large[rows, :] = product(table[0], table[1], rows, large)
            c_small[rows, :] = product(table[2], table[3], rows, small)

        for part in range(2):
            rows = pl.ds(part * KMAX, KMAX)
            down = jnp.where(KMAX - 1 - mode < kept_small, c_small[rows, :], 0.0)
            up = jnp.where(mode < kept_large, c_large[rows, :], 0.0)
            send_ref[s, part, pl.ds(0, KMAX), :] = up
            if start_small < KMAX:
                shared = KMAX - start_small
                send_ref[s, part, pl.ds(start_small, shared), :] = up[start_small:] + down[:shared]
            if start_small > 0:
                send_ref[s, part, pl.ds(KMAX, start_small), :] = down[KMAX - start_small :]
        exchange(s).start()

    for i in range(2, 4):
        split_table(i)

    @pl.loop(0, steps)
    def _(s):
        exchange(s).wait_recv()
        for part in range(2):
            rows = pl.ds(part * KMAX, KMAX)
            total = send_ref[s, part] + sign_ref[...] * recv_ref[s, part]
            up = jnp.where(mode < kept_large, total[:KMAX], 0.0)
            down = jnp.where(KMAX - 1 - mode < kept_small, total[start_small:], 0.0)
            large[rows, :] = jnp.concatenate(halves(up), axis=1)
            small[rows, :] = jnp.concatenate(halves(down), axis=1)

        @pl.loop(0, points // TILE)
        def _(t):
            rows = pl.ds(pl.multiple_of(t * TILE, TILE), TILE)
            result = jnp.concatenate(
                [
                    product(table[4], table[5], rows, large),
                    product(table[6], table[7], rows, small),
                ],
                axis=1,
            )
            high, low = halves(result)
            result = dot(high, gather_ref[...]) + dot(low, gather_ref[...])
            x_ref[2 * s, rows, :] = result[:, :LANES]
            x_ref[2 * s + 1, rows, :] = result[:, LANES:]

    @pl.loop(0, steps)
    def _(s):
        exchange(s).wait_send()


def exchange(length, collective_id, lines, host, spread, gather, kept):
    groups, points, lanes = lines.shape
    steps = groups // 2
    anywhere = pl.BlockSpec(memory_space=pl.ANY)
    inside = pl.BlockSpec(memory_space=pltpu.VMEM)
    dma = pltpu.SemaphoreType.DMA
    deep = max(points, 2 * KMAX)
    return pl.pallas_call(
        functools.partial(exchange_kernel, length),
        out_shape=pltpu.VMEM(lines.shape, jnp.float32),
        in_specs=[anywhere] * 5 + [inside] * 3,
        out_specs=inside,
        scratch_shapes=[pltpu.VMEM(t.shape, jnp.float32) for t in host]
        + [pltpu.VMEM(t.shape, jnp.bfloat16) for t in host for _ in range(2)]
        + [
            pltpu.VMEM((steps, 2, length, lanes), jnp.float32),
            pltpu.VMEM((steps, 2, length, lanes), jnp.float32),
            pltpu.VMEM((length, lanes), jnp.float32),
            pltpu.VMEM((deep, 2 * lanes), jnp.bfloat16),
            pltpu.VMEM((deep, 2 * lanes), jnp.bfloat16),
            pltpu.VMEM((2 * KMAX, lanes), jnp.float32),
            pltpu.VMEM((2 * KMAX, lanes), jnp.float32),
            dma((4,)),
            dma((steps,)),
            dma((steps,)),
            dma((steps,)),
        ],
        compiler_params=pltpu.CompilerParams(
            collective_id=collective_id,
            has_side_effects=True,
            vmem_limit_bytes=50 * 1024 * 1024,
        ),
        name="exchange_" + str(length),
    )(lines, *host, spread, gather, kept)


def paired(lines, count_table):
    nfields, shells, points, lanes = lines.shape
    whole = pl.BlockSpec(memory_space=pltpu.VMEM)
    spread, gather, kept, branch = pl.pallas_call(
        order_kernel,
        out_shape=(
            jax.ShapeDtypeStruct((2 * lanes, 2 * lanes), jnp.bfloat16),
            jax.ShapeDtypeStruct((2 * lanes, 2 * lanes), jnp.bfloat16),
            jax.ShapeDtypeStruct((1, 2 * lanes), jnp.int32),
            jax.ShapeDtypeStruct((1,), jnp.int32),
        ),
        in_specs=[whole],
        out_specs=(whole, whole, whole, pl.BlockSpec(memory_space=pltpu.SMEM)),
        name="order_rows",
    )(count_table)
    host = [jnp.asarray(t) for t in host_tables(points)]
    branches = [
        functools.partial(exchange, length, index) for index, length in enumerate(LENGTHS)
    ]
    grouped = lines.reshape(nfields * shells, points, lanes)
    result = lax.switch(branch[0], branches, grouped, host, spread, gather, kept)
    return result.reshape(lines.shape)


def on_device(fields, kept_counts):
    n_theta = lax.axis_size("theta")
    theta_index = lax.axis_index("theta")
    band_rows = fields.shape[3]
    caps = kept_counts.shape[0] // band_rows
    cap_bands = caps // 2
    count_table = kept_counts.reshape(caps, band_rows)
    low_side = theta_index < cap_bands
    high_side = theta_index >= n_theta - cap_bands
    position = jnp.where(low_side, theta_index, theta_index - (n_theta - 2 * cap_bands))
    position = jnp.clip(position, 0, caps - 1)
    row_counts = lax.dynamic_index_in_dim(count_table, position, 0, keepdims=False)
    fits = (
        lax.axis_size("phi") == 2
        and band_rows == LANES
        and fields.shape[0] * fields.shape[1] % 2 == 0
        and fields.shape[2] % TILE == 0
    )
    if fits:
        smoothed = paired(fields, count_table)
    else:
        smoothed = spectral(fields, row_counts)
    if n_theta == caps:
        return smoothed
    return jnp.where(jnp.logical_or(low_side, high_side), smoothed, fields)


def solution(mesh):
    placed = (P(None, "row", "phi", "theta"), P())
    return jax.shard_map(
        on_device,
        mesh=mesh,
        in_specs=placed,
        out_specs=P(None, "row", "phi", "theta"),
        check_vma=False,
    )
```

```python
import functools
import math

import jax
import jax.numpy as jnp
import numpy as np
from jax import lax
from jax.experimental import pallas as pl
from jax.experimental.pallas import tpu as pltpu
from jax.sharding import PartitionSpec as P

KMAX = 384
TILE = 128
LANES = 128
EIGHT = 8
LENGTHS = tuple(range(KMAX, 448, EIGHT)) + (456, 480, 528, 576, 2 * KMAX)


def tables(offset, span_rows, points, mode_count):
    azimuth = offset + jnp.arange(span_rows, dtype=jnp.int32)
    wavenumber = jnp.arange(mode_count, dtype=jnp.int32)
    phase_turns = azimuth[:, None] * wavenumber[None, :] % points
    angles = phase_turns.astype(jnp.float32) * (2.0 * math.pi / points)
    forward = jnp.concatenate([jnp.cos(angles), jnp.sin(angles)], axis=1)
    weight = jnp.where(wavenumber == 0, 1.0, 2.0).astype(jnp.float32) / points
    weight = jnp.concatenate([weight, weight])
    backward = (forward * weight[None, :]).T
    return (forward, backward)


def spectral(lines, row_counts):
    nfields, shells, local_points, rows_here = lines.shape
    n_phi = lax.axis_size("phi")
    points = local_points * n_phi
    highest = lax.Precision.HIGHEST
    groups = nfields * shells
    grouped = lines.reshape(groups, local_points, rows_here)
    line_counts = jnp.broadcast_to(row_counts[None, :], (groups, rows_here)).reshape(-1)
    phi_index = lax.axis_index("phi")
    forward, backward = tables(phi_index * local_points, local_points, points, KMAX)
    share_rows = forward.shape[1] // n_phi
    out = jnp.einsum(
        "pk,gpr->kgr", forward, grouped, precision=highest, preferred_element_type=jnp.float32
    )
    share = lax.psum_scatter(
        out.reshape(share_rows * lax.axis_size("phi"), groups * rows_here),
        "phi",
        scatter_dimension=0,
        tiled=True,
    )
    share_index = phi_index * share_rows + jnp.arange(share_rows, dtype=jnp.int32)
    keep = (share_index % KMAX)[:, None] < line_counts[None, :]
    masked = jnp.where(keep, share, 0.0)
    piece = lax.all_gather(masked, "phi", axis=0, tiled=True)
    stacked = piece.reshape(piece.shape[0], groups, rows_here)
    result = jnp.einsum(
        "kp,kgr->gpr", backward, stacked, precision=highest, preferred_element_type=jnp.float32
    )
    return result.reshape(lines.shape)


def halves(x):
    high = x.astype(jnp.bfloat16)
    return high, (x - high.astype(jnp.float32)).astype(jnp.bfloat16)


def host_tables(half):
    points = 2 * half
    azimuth = np.arange(half)
    mode = np.arange(KMAX)
    angle = (mode[:, None] * azimuth[None, :] % points) * (2.0 * math.pi / points)
    cos, sin = np.cos(angle), np.sin(angle)
    weight = (np.where(mode == 0, 1.0, 2.0) / points)[:, None]
    forward = np.concatenate([cos, sin])
    backward = np.concatenate([cos * weight, sin * weight]).T
    return [t.astype(np.float32) for t in (forward, backward)]


def order_kernel(all_ref, start_ref, kept_ref, branch_ref):
    def runs(counts):
        return ((counts + (EIGHT - 1)) // EIGHT).astype(jnp.float32)

    bands = all_ref.shape[0]
    n_theta = lax.axis_size("theta")
    theta_index = lax.axis_index("theta")
    position = jnp.where(
        theta_index < bands // 2, theta_index, theta_index - (n_theta - bands // 2 * 2)
    )
    position = jnp.clip(position, 0, bands - 1)
    own = all_ref[0:1, :]
    for band in range(1, bands):
        own = jnp.where(position == band, all_ref[band : band + 1, :], own)
    down = jnp.broadcast_to(runs(own), (LANES, LANES)).T
    lane = lax.broadcasted_iota(jnp.int32, (LANES, LANES), 1)
    line = lax.broadcasted_iota(jnp.int32, (LANES, LANES), 0)
    start = jnp.sum(jnp.where(line < lane, down, 0.0), axis=0, keepdims=True).astype(jnp.int32)
    start_ref[...] = jnp.concatenate([start, start], axis=1)
    kept_ref[...] = jnp.concatenate([own, own], axis=1)
    longest = jnp.max(jnp.sum(runs(all_ref[...]), axis=1, keepdims=True)).astype(jnp.int32)
    branch = jnp.int32(0)
    for length in LENGTHS[:-1]:
        branch += (longest > length // EIGHT * (LANES // 2)).astype(jnp.int32)
    branch_ref[0] = branch


def turn(x, amount):
    amount %= x.shape[0]
    return x if amount == 0 else jnp.concatenate([x[-amount:], x[:-amount]], axis=0)


def turn_lanes(x, runs, direction):
    for bit in range((x.shape[0] // EIGHT - 1).bit_length()):
        moved = turn(x, direction * (EIGHT << bit))
        x = jnp.where((runs >> bit) & 1 == 1, moved, x)
    return x


def padded(x):
    extra = -x.shape[0] % 16
    if extra == 0:
        return x
    return jnp.concatenate([x, jnp.zeros((extra, x.shape[1]), x.dtype)], axis=0)


def exchange_kernel(length, x_hbm, *refs):
    table_hbm = refs[:2]
    start_ref, kept_ref, x_ref = refs[2:5]
    staged, table = refs[5:7], refs[7:11]
    send_ref, recv_ref, high_ref, low_ref, coef_ref, wide_high, wide_low, columns = refs[11:19]
    table_sem, in_sem, send_sem, recv_sem = refs[19:]
    steps = x_ref.shape[0] // 2
    points = x_ref.shape[1]
    half = LANES // 2
    other = 1 - lax.axis_index("phi")

    def copy_in(s):
        pair = pl.ds(2 * s, 2)
        return pltpu.make_async_copy(x_hbm.at[pair], x_ref.at[pair], in_sem.at[s])

    def copy_table(i):
        return pltpu.make_async_copy(table_hbm[i], staged[i], table_sem.at[i])

    def split_table(i):
        copy_table(i).wait()

        @pl.loop(0, staged[i].shape[0] // TILE)
        def _(t):
            rows = pl.ds(pl.multiple_of(t * TILE, TILE), TILE)
            high, low = halves(staged[i][rows, :])
            table[2 * i][rows, :] = high
            table[2 * i + 1][rows, :] = low

    def exchange(s):
        return pltpu.make_async_remote_copy(
            src_ref=send_ref.at[s],
            dst_ref=recv_ref.at[s],
            send_sem=send_sem.at[s],
            recv_sem=recv_sem.at[s],
            device_id={"phi": other},
            device_id_type=pl.DeviceIdType.MESH,
        )

    copy_in(0).start()
    copy_table(0).start()
    barrier = pltpu.get_barrier_semaphore()
    pl.semaphore_signal(
        barrier, inc=1, device_id={"phi": other}, device_id_type=pl.DeviceIdType.MESH
    )

    @pl.loop(1, steps)
    def _(s):
        copy_in(s).start()

    copy_table(1).start()

    capacity = length // EIGHT
    start = start_ref[...]
    column = jnp.floor((start.astype(jnp.float32) + 0.5) * (1.0 / capacity)).astype(jnp.int32)
    place = (start - column * capacity)[:, :LANES]
    group = lax.broadcasted_iota(jnp.int32, (1, 2 * LANES), 1) // LANES
    column = column + group * half
    column = jnp.concatenate([column, column + 1], axis=1)
    index = lax.broadcasted_iota(jnp.int32, (LANES, 4 * LANES), 0)
    columns[...] = jnp.where(index == column, 1.0, 0.0).astype(jnp.bfloat16)
    kept = kept_ref[:, :LANES]
    mode = lax.broadcasted_iota(jnp.int32, (KMAX, LANES), 0)
    row = lax.broadcasted_iota(jnp.int32, (length, LANES), 0)

    def dot(a, b):
        return jnp.dot(a, b, preferred_element_type=jnp.float32)

    def dot_back(a, b):
        return lax.dot_general(a, b, (((1,), (1,)), ((), ())), preferred_element_type=jnp.float32)

    def product(i, rows):
        high, low = table[2 * i], table[2 * i + 1]
        total = dot(high[rows, :], low_ref[...]) + dot(low[rows, :], high_ref[...])
        return total + dot(high[rows, :], high_ref[...])

    split_table(0)
    pl.semaphore_wait(barrier, 1)

    @pl.loop(0, steps)
    def _(s):
        copy_in(s).wait()

        @pl.loop(0, points // TILE)
        def _(t):
            rows = pl.ds(pl.multiple_of(t * TILE, TILE), TILE)
            both = jnp.concatenate([x_ref[2 * s, rows, :], x_ref[2 * s + 1, rows, :]], axis=1)
            high, low = halves(both)
            high_ref[rows, :] = high
            low_ref[rows, :] = low

        @pl.loop(0, 2 * KMAX // TILE)
        def _(t):
            rows = pl.ds(pl.multiple_of(t * TILE, TILE), TILE)
            coef_ref[rows, :] = product(0, rows)

        for part in range(2):
            for g in range(2):
                lanes = pl.ds(g * LANES, LANES)
                lanes_on = pl.ds((2 + g) * LANES, LANES)
                x = jnp.where(mode < kept, coef_ref[pl.ds(part * KMAX, KMAX), lanes], 0.0)
                if length > KMAX:
                    x = jnp.concatenate([x, jnp.zeros((length - KMAX, LANES), jnp.float32)], axis=0)
                x = turn_lanes(x, place, 1)
                here = row >= place * EIGHT
                for lane_set, piece in (
                    (lanes, jnp.where(here, x, 0.0)),
                    (lanes_on, jnp.where(here, 0.0, x)),
                ):
                    high, low = halves(padded(piece))
                    wide_high[:, lane_set] = high
                    wide_low[:, lane_set] = low
            packed = dot_back(wide_high[...], columns[...])
            packed = packed + dot_back(wide_low[...], columns[...])
            send_ref[s, part] = packed[:length]
        exchange(s).start()

    split_table(1)

    @pl.loop(0, steps)
    def _(s):
        exchange(s).wait_recv()
        sign = 1.0 - 2.0 * (row % 2).astype(jnp.float32)
        for part in range(2):
            high, low = halves(padded(send_ref[s, part] + sign * recv_ref[s, part]))
            for g in range(2):
                here = row >= place * EIGHT
                first = columns[:, g * LANES : (g + 1) * LANES]
                second = columns[:, (2 + g) * LANES : (3 + g) * LANES]
                first = (dot(high, first) + dot(low, first))[:length]
                second = (dot(high, second) + dot(low, second))[:length]
                x = jnp.where(here, first, second)
                x = turn_lanes(x, place, -1)[:KMAX]
                x_high, x_low = halves(jnp.where(mode < kept, x, 0.0))
                rows, lanes = pl.ds(part * KMAX, KMAX), pl.ds(g * LANES, LANES)
                high_ref[rows, lanes] = x_high
                low_ref[rows, lanes] = x_low

        @pl.loop(0, points // TILE)
        def _(t):
            rows = pl.ds(pl.multiple_of(t * TILE, TILE), TILE)
            result = product(1, rows)
            x_ref[2 * s, rows, :] = result[:, :LANES]
            x_ref[2 * s + 1, rows, :] = result[:, LANES:]

    @pl.loop(0, steps)
    def _(s):
        exchange(s).wait_send()


def exchange(length, collective_id, lines, host, start, kept):
    groups, points, lanes = lines.shape
    steps = groups // 2
    anywhere = pl.BlockSpec(memory_space=pl.ANY)
    inside = pl.BlockSpec(memory_space=pltpu.VMEM)
    dma = pltpu.SemaphoreType.DMA
    deep = max(points, 2 * KMAX)
    return pl.pallas_call(
        functools.partial(exchange_kernel, length),
        out_shape=pltpu.VMEM(lines.shape, jnp.float32),
        in_specs=[anywhere] * 3 + [inside] * 2,
        out_specs=inside,
        scratch_shapes=[pltpu.VMEM(t.shape, jnp.float32) for t in host]
        + [pltpu.VMEM(t.shape, jnp.bfloat16) for t in host for _ in range(2)]
        + [
            pltpu.VMEM((steps, 2, length, lanes), jnp.float32),
            pltpu.VMEM((steps, 2, length, lanes), jnp.float32),
            pltpu.VMEM((deep, 2 * lanes), jnp.bfloat16),
            pltpu.VMEM((deep, 2 * lanes), jnp.bfloat16),
            pltpu.VMEM((2 * KMAX, 2 * lanes), jnp.float32),
            pltpu.VMEM((-(-length // 16) * 16, 4 * lanes), jnp.bfloat16),
            pltpu.VMEM((-(-length // 16) * 16, 4 * lanes), jnp.bfloat16),
            pltpu.VMEM((lanes, 4 * lanes), jnp.bfloat16),
            dma((2,)),
            dma((steps,)),
            dma((steps,)),
            dma((steps,)),
        ],
        compiler_params=pltpu.CompilerParams(
            collective_id=collective_id,
            has_side_effects=True,
            vmem_limit_bytes=50 * 1024 * 1024,
        ),
        name="exchange_" + str(length),
    )(lines, *host, start, kept)


def paired(lines, count_table):
    nfields, shells, points, lanes = lines.shape
    whole = pl.BlockSpec(memory_space=pltpu.VMEM)
    start, kept, branch = pl.pallas_call(
        order_kernel,
        out_shape=(
            jax.ShapeDtypeStruct((1, 2 * lanes), jnp.int32),
            jax.ShapeDtypeStruct((1, 2 * lanes), jnp.int32),
            jax.ShapeDtypeStruct((1,), jnp.int32),
        ),
        in_specs=[whole],
        out_specs=(whole, whole, pl.BlockSpec(memory_space=pltpu.SMEM)),
        name="order_rows",
    )(count_table)
    host = [jnp.asarray(t) for t in host_tables(points)]
    branches = [
        functools.partial(exchange, length, index) for index, length in enumerate(LENGTHS)
    ]
    grouped = lines.reshape(nfields * shells, points, lanes)
    result = lax.switch(branch[0], branches, grouped, host, start, kept)
    return result.reshape(lines.shape)


def on_device(fields, kept_counts):
    n_theta = lax.axis_size("theta")
    theta_index = lax.axis_index("theta")
    band_rows = fields.shape[3]
    caps = kept_counts.shape[0] // band_rows
    cap_bands = caps // 2
    count_table = kept_counts.reshape(caps, band_rows)
    low_side = theta_index < cap_bands
    high_side = theta_index >= n_theta - cap_bands
    position = jnp.where(low_side, theta_index, theta_index - (n_theta - 2 * cap_bands))
    position = jnp.clip(position, 0, caps - 1)
    row_counts = lax.dynamic_index_in_dim(count_table, position, 0, keepdims=False)
    fits = (
        lax.axis_size("phi") == 2
        and band_rows == LANES
        and fields.shape[0] * fields.shape[1] % 2 == 0
        and fields.shape[2] == 2 * KMAX
    )
    if fits:
        smoothed = paired(fields, count_table)
    else:
        smoothed = spectral(fields, row_counts)
    if n_theta == caps:
        return smoothed
    return jnp.where(jnp.logical_or(low_side, high_side), smoothed, fields)


def solution(mesh):
    placed = (P(None, "row", "phi", "theta"), P())
    return jax.shard_map(
        on_device,
        mesh=mesh,
        in_specs=placed,
        out_specs=P(None, "row", "phi", "theta"),
        check_vma=False,
    )
```

```python
import functools
import math

import jax
import jax.numpy as jnp
import numpy as np
from jax import lax
from jax.experimental import pallas as pl
from jax.experimental.pallas import tpu as pltpu
from jax.sharding import PartitionSpec as P

KMAX = 384
TILE = 128
LANES = 128
EIGHT = 8
LENGTHS = tuple(range(KMAX, 448, EIGHT)) + (456, 480, 528, 576, 2 * KMAX)


def tables(offset, span_rows, points, mode_count):
    azimuth = offset + jnp.arange(span_rows, dtype=jnp.int32)
    wavenumber = jnp.arange(mode_count, dtype=jnp.int32)
    phase_turns = azimuth[:, None] * wavenumber[None, :] % points
    angles = phase_turns.astype(jnp.float32) * (2.0 * math.pi / points)
    forward = jnp.concatenate([jnp.cos(angles), jnp.sin(angles)], axis=1)
    weight = jnp.where(wavenumber == 0, 1.0, 2.0).astype(jnp.float32) / points
    weight = jnp.concatenate([weight, weight])
    backward = (forward * weight[None, :]).T
    return (forward, backward)


def spectral(lines, row_counts):
    nfields, shells, local_points, rows_here = lines.shape
    n_phi = lax.axis_size("phi")
    points = local_points * n_phi
    highest = lax.Precision.HIGHEST
    groups = nfields * shells
    grouped = lines.reshape(groups, local_points, rows_here)
    line_counts = jnp.broadcast_to(row_counts[None, :], (groups, rows_here)).reshape(-1)
    phi_index = lax.axis_index("phi")
    forward, backward = tables(phi_index * local_points, local_points, points, KMAX)
    share_rows = forward.shape[1] // n_phi
    out = jnp.einsum(
        "pk,gpr->kgr", forward, grouped, precision=highest, preferred_element_type=jnp.float32
    )
    share = lax.psum_scatter(
        out.reshape(share_rows * lax.axis_size("phi"), groups * rows_here),
        "phi",
        scatter_dimension=0,
        tiled=True,
    )
    share_index = phi_index * share_rows + jnp.arange(share_rows, dtype=jnp.int32)
    keep = (share_index % KMAX)[:, None] < line_counts[None, :]
    masked = jnp.where(keep, share, 0.0)
    piece = lax.all_gather(masked, "phi", axis=0, tiled=True)
    stacked = piece.reshape(piece.shape[0], groups, rows_here)
    result = jnp.einsum(
        "kp,kgr->gpr", backward, stacked, precision=highest, preferred_element_type=jnp.float32
    )
    return result.reshape(lines.shape)


def halves(x):
    high = x.astype(jnp.bfloat16)
    return high, (x - high.astype(jnp.float32)).astype(jnp.bfloat16)


def host_tables(half):
    points = 2 * half
    azimuth = np.arange(half)
    mode = np.arange(KMAX)
    angle = (mode[:, None] * azimuth[None, :] % points) * (2.0 * math.pi / points)
    cos, sin = np.cos(angle), np.sin(angle)
    weight = (np.where(mode == 0, 1.0, 2.0) / points)[:, None]
    forward = np.concatenate([cos, sin])
    backward = np.concatenate([cos * weight, sin * weight]).T
    return [t.astype(np.float32) for t in (forward, backward)]


def order_kernel(all_ref, start_ref, kept_ref, branch_ref):
    def runs(counts):
        return ((counts + (EIGHT - 1)) // EIGHT).astype(jnp.float32)

    bands = all_ref.shape[0]
    n_theta = lax.axis_size("theta")
    theta_index = lax.axis_index("theta")
    position = jnp.where(
        theta_index < bands // 2, theta_index, theta_index - (n_theta - bands // 2 * 2)
    )
    position = jnp.clip(position, 0, bands - 1)
    own = all_ref[0:1, :]
    for band in range(1, bands):
        own = jnp.where(position == band, all_ref[band : band + 1, :], own)
    down = jnp.broadcast_to(runs(own), (LANES, LANES)).T
    lane = lax.broadcasted_iota(jnp.int32, (LANES, LANES), 1)
    line = lax.broadcasted_iota(jnp.int32, (LANES, LANES), 0)
    start = jnp.sum(jnp.where(line < lane, down, 0.0), axis=0, keepdims=True).astype(jnp.int32)
    start_ref[...] = jnp.concatenate([start, start], axis=1)
    kept_ref[...] = jnp.concatenate([own, own], axis=1)
    longest = jnp.max(jnp.sum(runs(all_ref[...]), axis=1, keepdims=True)).astype(jnp.int32)
    branch = jnp.int32(0)
    for length in LENGTHS[:-1]:
        branch += (longest > length // EIGHT * (LANES // 2)).astype(jnp.int32)
    branch_ref[0] = branch


def turn(x, amount):
    amount %= x.shape[0]
    return x if amount == 0 else jnp.concatenate([x[-amount:], x[:-amount]], axis=0)


def turn_lanes(x, runs, direction):
    for bit in range((x.shape[0] // EIGHT - 1).bit_length()):
        moved = turn(x, direction * (EIGHT << bit))
        x = jnp.where((runs >> bit) & 1 == 1, moved, x)
    return x


def padded(x):
    extra = -x.shape[0] % 16
    if extra == 0:
        return x
    return jnp.concatenate([x, jnp.zeros((extra, x.shape[1]), x.dtype)], axis=0)


def exchange_kernel(length, x_hbm, *refs):
    table_hbm = refs[:2]
    start_ref, kept_ref, x_ref = refs[2:5]
    staged, table = refs[5:7], refs[7:11]
    send_ref, recv_ref, high_ref, low_ref, coef_ref, wide_high, wide_low, columns = refs[11:19]
    table_sem, in_sem, send_sem, recv_sem = refs[19:]
    steps = x_ref.shape[0] // 2
    points = x_ref.shape[1]
    half = LANES // 2
    other = 1 - lax.axis_index("phi")

    def copy_in(s):
        pair = pl.ds(2 * s, 2)
        return pltpu.make_async_copy(x_hbm.at[pair], x_ref.at[pair], in_sem.at[s])

    def copy_table(i):
        return pltpu.make_async_copy(table_hbm[i], staged[i], table_sem.at[i])

    def split_table(i):
        copy_table(i).wait()

        @pl.loop(0, staged[i].shape[0] // TILE)
        def _(t):
            rows = pl.ds(pl.multiple_of(t * TILE, TILE), TILE)
            high, low = halves(staged[i][rows, :])
            table[2 * i][rows, :] = high
            table[2 * i + 1][rows, :] = low

    def exchange(s, part):
        return pltpu.make_async_remote_copy(
            src_ref=send_ref.at[s, part],
            dst_ref=recv_ref.at[s, part],
            send_sem=send_sem.at[s, part],
            recv_sem=recv_sem.at[s, part],
            device_id={"phi": other},
            device_id_type=pl.DeviceIdType.MESH,
        )

    copy_in(0).start()
    copy_table(0).start()
    barrier = pltpu.get_barrier_semaphore()
    pl.semaphore_signal(
        barrier, inc=1, device_id={"phi": other}, device_id_type=pl.DeviceIdType.MESH
    )

    @pl.loop(1, steps)
    def _(s):
        copy_in(s).start()

    copy_table(1).start()

    capacity = length // EIGHT
    start = start_ref[...]
    column = jnp.floor((start.astype(jnp.float32) + 0.5) * (1.0 / capacity)).astype(jnp.int32)
    place = (start - column * capacity)[:, :LANES]
    group = lax.broadcasted_iota(jnp.int32, (1, 2 * LANES), 1) // LANES
    column = column + group * half
    column = jnp.concatenate([column, column + 1], axis=1)
    index = lax.broadcasted_iota(jnp.int32, (LANES, 4 * LANES), 0)
    columns[...] = jnp.where(index == column, 1.0, 0.0).astype(jnp.bfloat16)
    kept = kept_ref[:, :LANES]
    mode = lax.broadcasted_iota(jnp.int32, (KMAX, LANES), 0)
    row = lax.broadcasted_iota(jnp.int32, (length, LANES), 0)

    def dot(a, b):
        return jnp.dot(a, b, preferred_element_type=jnp.float32)

    def dot_back(a, b):
        return lax.dot_general(a, b, (((1,), (1,)), ((), ())), preferred_element_type=jnp.float32)

    def product(i, rows):
        high, low = table[2 * i], table[2 * i + 1]
        total = dot(high[rows, :], low_ref[...]) + dot(low[rows, :], high_ref[...])
        return total + dot(high[rows, :], high_ref[...])

    split_table(0)
    pl.semaphore_wait(barrier, 1)

    @pl.loop(0, steps)
    def _(s):
        copy_in(s).wait()

        @pl.loop(0, points // TILE)
        def _(t):
            rows = pl.ds(pl.multiple_of(t * TILE, TILE), TILE)
            both = jnp.concatenate([x_ref[2 * s, rows, :], x_ref[2 * s + 1, rows, :]], axis=1)
            high, low = halves(both)
            high_ref[rows, :] = high
            low_ref[rows, :] = low

        for part in range(2):

            @pl.loop(part * KMAX // TILE, (part + 1) * KMAX // TILE)
            def _(t):
                rows = pl.ds(pl.multiple_of(t * TILE, TILE), TILE)
                coef_ref[rows, :] = product(0, rows)

            for g in range(2):
                lanes = pl.ds(g * LANES, LANES)
                lanes_on = pl.ds((2 + g) * LANES, LANES)
                x = jnp.where(mode < kept, coef_ref[pl.ds(part * KMAX, KMAX), lanes], 0.0)
                if length > KMAX:
                    x = jnp.concatenate([x, jnp.zeros((length - KMAX, LANES), jnp.float32)], axis=0)
                x = turn_lanes(x, place, 1)
                here = row >= place * EIGHT
                for lane_set, piece in (
                    (lanes, jnp.where(here, x, 0.0)),
                    (lanes_on, jnp.where(here, 0.0, x)),
                ):
                    high, low = halves(padded(piece))
                    wide_high[:, lane_set] = high
                    wide_low[:, lane_set] = low
            packed = dot_back(wide_high[...], columns[...])
            packed = packed + dot_back(wide_low[...], columns[...])
            send_ref[s, part] = packed[:length]
            exchange(s, part).start()

    split_table(1)

    @pl.loop(0, steps)
    def _(s):
        sign = 1.0 - 2.0 * (row % 2).astype(jnp.float32)
        for part in range(2):
            exchange(s, part).wait_recv()
            high, low = halves(padded(send_ref[s, part] + sign * recv_ref[s, part]))
            for g in range(2):
                here = row >= place * EIGHT
                first = columns[:, g * LANES : (g + 1) * LANES]
                second = columns[:, (2 + g) * LANES : (3 + g) * LANES]
                first = (dot(high, first) + dot(low, first))[:length]
                second = (dot(high, second) + dot(low, second))[:length]
                x = jnp.where(here, first, second)
                x = turn_lanes(x, place, -1)[:KMAX]
                x_high, x_low = halves(jnp.where(mode < kept, x, 0.0))
                rows, lanes = pl.ds(part * KMAX, KMAX), pl.ds(g * LANES, LANES)
                high_ref[rows, lanes] = x_high
                low_ref[rows, lanes] = x_low

        @pl.loop(0, points // TILE)
        def _(t):
            rows = pl.ds(pl.multiple_of(t * TILE, TILE), TILE)
            result = product(1, rows)
            x_ref[2 * s, rows, :] = result[:, :LANES]
            x_ref[2 * s + 1, rows, :] = result[:, LANES:]

    @pl.loop(0, steps)
    def _(s):
        for part in range(2):
            exchange(s, part).wait_send()


def exchange(length, collective_id, lines, host, start, kept):
    groups, points, lanes = lines.shape
    steps = groups // 2
    anywhere = pl.BlockSpec(memory_space=pl.ANY)
    inside = pl.BlockSpec(memory_space=pltpu.VMEM)
    dma = pltpu.SemaphoreType.DMA
    deep = max(points, 2 * KMAX)
    return pl.pallas_call(
        functools.partial(exchange_kernel, length),
        out_shape=pltpu.VMEM(lines.shape, jnp.float32),
        in_specs=[anywhere] * 3 + [inside] * 2,
        out_specs=inside,
        scratch_shapes=[pltpu.VMEM(t.shape, jnp.float32) for t in host]
        + [pltpu.VMEM(t.shape, jnp.bfloat16) for t in host for _ in range(2)]
        + [
            pltpu.VMEM((steps, 2, length, lanes), jnp.float32),
            pltpu.VMEM((steps, 2, length, lanes), jnp.float32),
            pltpu.VMEM((deep, 2 * lanes), jnp.bfloat16),
            pltpu.VMEM((deep, 2 * lanes), jnp.bfloat16),
            pltpu.VMEM((2 * KMAX, 2 * lanes), jnp.float32),
            pltpu.VMEM((-(-length // 16) * 16, 4 * lanes), jnp.bfloat16),
            pltpu.VMEM((-(-length // 16) * 16, 4 * lanes), jnp.bfloat16),
            pltpu.VMEM((lanes, 4 * lanes), jnp.bfloat16),
            dma((2,)),
            dma((steps,)),
            dma((steps, 2)),
            dma((steps, 2)),
        ],
        compiler_params=pltpu.CompilerParams(
            collective_id=collective_id,
            has_side_effects=True,
            vmem_limit_bytes=50 * 1024 * 1024,
        ),
        name="exchange_" + str(length),
    )(lines, *host, start, kept)


def paired(lines, count_table):
    nfields, shells, points, lanes = lines.shape
    whole = pl.BlockSpec(memory_space=pltpu.VMEM)
    start, kept, branch = pl.pallas_call(
        order_kernel,
        out_shape=(
            jax.ShapeDtypeStruct((1, 2 * lanes), jnp.int32),
            jax.ShapeDtypeStruct((1, 2 * lanes), jnp.int32),
            jax.ShapeDtypeStruct((1,), jnp.int32),
        ),
        in_specs=[whole],
        out_specs=(whole, whole, pl.BlockSpec(memory_space=pltpu.SMEM)),
        name="order_rows",
    )(count_table)
    host = [jnp.asarray(t) for t in host_tables(points)]
    branches = [
        functools.partial(exchange, length, index) for index, length in enumerate(LENGTHS)
    ]
    grouped = lines.reshape(nfields * shells, points, lanes)
    result = lax.switch(branch[0], branches, grouped, host, start, kept)
    return result.reshape(lines.shape)


def on_device(fields, kept_counts):
    n_theta = lax.axis_size("theta")
    theta_index = lax.axis_index("theta")
    band_rows = fields.shape[3]
    caps = kept_counts.shape[0] // band_rows
    cap_bands = caps // 2
    count_table = kept_counts.reshape(caps, band_rows)
    low_side = theta_index < cap_bands
    high_side = theta_index >= n_theta - cap_bands
    position = jnp.where(low_side, theta_index, theta_index - (n_theta - 2 * cap_bands))
    position = jnp.clip(position, 0, caps - 1)
    row_counts = lax.dynamic_index_in_dim(count_table, position, 0, keepdims=False)
    fits = (
        lax.axis_size("phi") == 2
        and band_rows == LANES
        and fields.shape[0] * fields.shape[1] % 2 == 0
        and fields.shape[2] == 2 * KMAX
    )
    if fits:
        smoothed = paired(fields, count_table)
    else:
        smoothed = spectral(fields, row_counts)
    if n_theta == caps:
        return smoothed
    return jnp.where(jnp.logical_or(low_side, high_side), smoothed, fields)


def solution(mesh):
    placed = (P(None, "row", "phi", "theta"), P())
    return jax.shard_map(
        on_device,
        mesh=mesh,
        in_specs=placed,
        out_specs=P(None, "row", "phi", "theta"),
        check_vma=False,
    )
```
